32 devices in a mesh: grp: 4 (over y, x), dev: 8 (over z, core).
Axes of the slice: x: 2, y: 2, z: 4, core: 2. Of those that a mesh axis runs over, the one named last changes fastest.
Arguments:
- basis: float32 [512, 64, 1024], P(('grp', 'dev')), may hold values from -0.25 to 0.25
- leaf_transfer: float32 [512, 4096], P(('grp', 'dev')), may hold values from -0.75 to 1.75, as said below
- upper_transfer: float32 [256, 4096], P(('grp', 'dev')), may hold values from -0.75 to 1.75, as said below
- coupling: float32 [4096, 4096], P(('grp', 'dev')), may hold values from -6 to 6
- row_leaf: int32 [4096], P(('grp', 'dev')), may hold values from 0 to 15
- col_dev: int32 [4096, 1], P(('grp', 'dev')), may hold values from 0 to 31; in each aligned block of 128 rows (0 to 127, 128 to 255, ...) at most 8 rows name the same one
- col_leaf: int32 [4096], P(('grp', 'dev')), may hold values from 0 to 15
Outputs:
- ortho_basis: float32 [512, 64, 1024], P(('grp', 'dev'))
- leaf_transfer_out: float32 [512, 4096], P(('grp', 'dev'))
- upper_transfer_out: float32 [256, 4096], P(('grp', 'dev'))
- coupling_out: float32 [4096, 4096], P(('grp', 'dev'))
The draws below stay inside these ranges and needn't reach their ends.
Inputs may be any that keep to these rules, and one draw needn't show every extreme that they name: `col_dev`: among the 128 blocks of one device no device index appears more than 8 times, and some index appears exactly 8 times on some device. `leaf_transfer`: each row is a K x K matrix near the identity. `upper_transfer`: each row is a K x K matrix near the identity.
All inputs are finite; a program needn't handle non-finite values.
Results may differ from the reference program's by a relative error of at most 0.0003.
Values sent between devices are 32-bit elements; how exact they have to be, the bound alone decides.
A program may use at most 128 MiB of HBM per device.

```python
import math
import jax
import jax.numpy as jnp
import numpy as np
from jax import lax

K = 64
LEAF = 1024
LEAF_DEV = 16
BLK_DEV = 128
NLEAF = 512
NL1 = 256
SPAN = 64
NBLK = 4096
CAP = 8
DEVICES = 32


def near_identity(key, count, width, salt):
    noise_key = jax.random.fold_in(key, salt)
    noise = jnp.clip(jax.random.normal(noise_key, (count, width, width), jnp.float32), -6.0, 6.0)
    spread = 0.5 / width ** 0.5
    mats = jnp.eye(width, dtype=jnp.float32)[None] + spread * noise
    return mats.reshape(count, width * width)


def draw_leaf_transfer(key, part):
    return near_identity(key, NLEAF, K, 11)


def draw_upper_transfer(key, part):
    return near_identity(key, NL1, K, 23)


def touch_ends(array, stream_key, smallest, top_value):
    index_at = [jax.random.randint(jax.random.fold_in(stream_key, axis), (), 0, length) for axis, length in enumerate(array.shape)]
    widest = array.shape.index(max(array.shape))
    next_to = index_at[:widest] + [(index_at[widest] + 1) % array.shape[widest]] + index_at[widest + 1:]
    return array.at[tuple(index_at)].set(smallest).at[tuple(next_to)].set(top_value)


def block_levels(own_key, shape, pieces, low, top_value):
    def one(position, parts):
        draws = jax.random.uniform(jax.random.fold_in(jax.random.fold_in(own_key, 6), position), (parts,), jnp.float32, low / len(pieces), top_value / len(pieces))
        return jnp.repeat(jnp.exp(draws), shape[position] // parts).reshape((-1,) + (1,) * (len(shape) - position - 1))

    level = one(*pieces[0])
    for cut in pieces[1:]:
        level = level * one(*cut)
    return level


def routed_block(rng, own, number, rows, count, top, limit, skew):
    sequence = jax.random.permutation(rng, count)
    heavy_load, common = portions_of(count, rows * top, limit, skew, True), portions_of(count, rows * top, limit, skew, False)
    places = jnp.arange(count)

    def named(lengths, turn):
        used = int((lengths > 0).sum())
        fixed = max(1, used // 4)
        moved = fixed + (places - fixed + turn * (used - fixed)) % max(1, count - fixed)
        return jnp.zeros((count,), jnp.int32).at[sequence[jnp.where(places < fixed, places, moved)]].set(jnp.asarray(lengths, jnp.int32))

    lengths = jnp.where(number % 4 == 0, named(heavy_load, number // 4), named(common, number - number // 4 - 1))
    mixed = jax.random.permutation(jax.random.fold_in(own, 3), count)
    giver, taker = mixed[0:count // 2 * 2:2], mixed[1:count // 2 * 2:2]
    slack = jnp.minimum(lengths[giver] - 1, limit - lengths[taker]) // 2
    slack = jnp.where((giver == sequence[0]) | (taker == sequence[0]) | (lengths[taker] == 0), 0, jnp.maximum(slack, 0))
    moved = jax.random.randint(jax.random.fold_in(own, 4), (count // 2,), 0, 1 << 20) % (slack + 1)
    lengths = lengths.at[giver].add(-moved).at[taker].add(moved)
    members = jnp.searchsorted(jnp.cumsum(lengths), jnp.arange(rows * top), side="right").astype(jnp.int32)
    listing = members.reshape(top, rows).T
    listing = listing[jax.random.permutation(jax.random.fold_in(own, 1), rows)]
    turn = jax.random.randint(jax.random.fold_in(own, 2), (rows, 1), 0, top)
    return jnp.take_along_axis(listing, (jnp.arange(top)[None, :] + turn) % top, axis=1)


def portions_of(count, total, bound, skew, full):
    weights = [(1 << 20) // math.isqrt(standing ** skew) + 1 for standing in range(1, count + 1)]
    largest = bound if full else min(bound, max(-(-total // count), total * weights[0] // sum(weights)))
    least = 1 if total - largest >= count - 1 else 0
    given, rest = [largest] + [least] * (count - 1), total - largest - least * (count - 1)
    while rest > 0:
        candidates = [i for i in range(1, count) if given[i] < largest] or [i for i in range(1, count) if given[i] < bound]
        whole, remaining = sum([weights[i] for i in candidates]), rest
        for i in candidates:
            extra = min(bound - given[i], max(1, remaining * weights[i] // whole), rest)
            given[i] = given[i] + extra
            rest = rest - extra
    return np.array(given)


def scatter_about(key, extent, scale, limit, pieces=(), kind=jnp.bfloat16):
    gain = block_levels(key, extent, pieces, -0.22, 0.18) if pieces else 1.0
    drawn = jax.random.normal(key, extent, jnp.float32) * scale * gain
    return jnp.minimum(jnp.maximum(drawn, -limit), limit).astype(kind)


def setup_inputs(seed: int = 0) -> dict:
    splits = jax.random.split(jax.random.key(seed), 8)
    basis = scatter_about(splits[0], (NLEAF, K, LEAF), 0.03125, 0.25, ((0, 32),), jnp.float32)
    leaf_transfer = draw_leaf_transfer(jax.random.fold_in(splits[7], 71), 0)
    upper_transfer = draw_upper_transfer(jax.random.fold_in(splits[7], 71), 0)
    coupling = scatter_about(splits[3], (NBLK, K * K), 1.0, 6.0, ((0, 32),), jnp.float32)
    row_leaf = touch_ends(jax.random.randint(splits[4], (NBLK,), 0, LEAF_DEV), jax.random.fold_in(splits[4], 1), 0, LEAF_DEV - 1).astype(jnp.int32)
    col_dev_keys = jax.random.split(jax.random.fold_in(splits[5], 1), NBLK // BLK_DEV)
    col_dev_turns = jax.random.permutation(jax.random.fold_in(splits[5], 3), NBLK // BLK_DEV)
    col_dev = jax.vmap(lambda own, number: routed_block(jax.random.fold_in(splits[5], 2), own, number, BLK_DEV, DEVICES, 1, CAP, 2))(col_dev_keys, col_dev_turns).reshape((NBLK, 1))
    col_leaf = touch_ends(jax.random.randint(splits[6], (NBLK,), 0, LEAF_DEV), jax.random.fold_in(splits[6], 1), 0, LEAF_DEV - 1).astype(jnp.int32)
    return dict(basis=basis, leaf_transfer=leaf_transfer, upper_transfer=upper_transfer, coupling=coupling, row_leaf=row_leaf, col_dev=col_dev, col_leaf=col_leaf)


exact_mode = lax.Precision.HIGHEST

def left_solve(lower, mats):
    return lax.linalg.triangular_solve(lower, mats, left_side=True, lower=True)

def right_solve(lower, mats):
    return lax.linalg.triangular_solve(lower, mats, left_side=False, lower=True, transpose_a=True)

def transpose_mul(first, second):
    return jnp.einsum('nji,njk->nik', first, second, precision=exact_mode)

def reference(basis, leaf_transfer, upper_transfer, coupling, row_leaf, col_dev, col_leaf):
    leaves, width, points = basis.shape
    gram = jnp.einsum('nkp,njp->nkj', basis, basis, precision=exact_mode)
    lower = jnp.linalg.cholesky(gram)
    ortho_basis = left_solve(lower, basis) * math.sqrt(points)
    lifted = transpose_mul(lower, leaf_transfer.reshape(leaves, width, width))
    inner = transpose_mul(lifted, lifted)
    lower_one = jnp.linalg.cholesky(inner.reshape(leaves // 2, 2, width, width).sum(axis=1))
    new_leaf = right_solve(jnp.repeat(lower_one, 2, axis=0), lifted)
    clusters = leaves // 2
    raised = transpose_mul(lower_one, upper_transfer.reshape(clusters, width, width))
    inner_up = transpose_mul(raised, raised)
    summed = inner_up.reshape(clusters // (2 * SPAN), 2, SPAN, width, width).sum(axis=1)
    lower_two = jnp.linalg.cholesky(summed)
    lower_two = jnp.broadcast_to(lower_two[:, None], (clusters // (2 * SPAN), 2, SPAN, width, width)).reshape(clusters, width, width)
    new_upper = right_solve(lower_two, raised)
    owners = NBLK // BLK_DEV
    upper_leaf = jnp.swapaxes(lower, 1, 2)

    def one_owner(index):
        start = (index * BLK_DEV).astype(jnp.int32)
        blocks = lax.dynamic_slice_in_dim(coupling, start, BLK_DEV, 0).reshape(BLK_DEV, width, width)
        rows = lax.dynamic_slice_in_dim(row_leaf, start, BLK_DEV, 0) + index * LEAF_DEV
        dests = lax.dynamic_slice_in_dim(col_dev[:, 0], start, BLK_DEV, 0)
        cols = dests * LEAF_DEV + lax.dynamic_slice_in_dim(col_leaf, start, BLK_DEV, 0)
        row_factor = jnp.take(upper_leaf, rows.astype(jnp.int32), axis=0)
        col_factor = jnp.take(upper_leaf, cols.astype(jnp.int32), axis=0)
        left = jnp.einsum('bij,bjk->bik', row_factor, blocks, precision=exact_mode)
        done = jnp.einsum('bij,bkj->bik', left, col_factor, precision=exact_mode)
        return done.reshape(BLK_DEV, width * width)
    coupling_out = lax.map(one_owner, jnp.arange(owners, dtype=jnp.int32)).reshape(NBLK, width * width)
    return (ortho_basis, new_leaf.reshape(leaves, width * width), new_upper.reshape(clusters, width * width), coupling_out)
```

```python
import functools
import math

import jax
import jax.numpy as jnp
from jax import lax
from jax.experimental import pallas as pl
from jax.experimental.pallas import tpu as pltpu
from jax.sharding import PartitionSpec as P

GROUP = 8
NN = (((1,), (0,)), ((), ()))
NT = (((1,), (1,)), ((), ()))
TN = (((0,), (0,)), ((), ()))
VMEM_BYTES = 56 * 1024 * 1024


def split(x):
    high = x.astype(jnp.bfloat16)
    return high, (x - high.astype(jnp.float32)).astype(jnp.bfloat16)


def mul(first, second, dims):
    return lax.dot_general(first, second, dims, preferred_element_type=jnp.float32)


def split_mul(first, second, dims):
    return (
        mul(first[0], second[1], dims)
        + mul(first[1], second[0], dims)
        + mul(first[0], second[0], dims)
    )


def exact_mul(first, second, dims):
    return split_mul(split(first), split(second), dims)


def eliminate(tiles):
    tiles = list(tiles)
    count, eight, lanes = tiles[0].shape
    row_of = lax.broadcasted_iota(jnp.int32, (1, eight, 1), 1)
    for j in range(len(tiles) * eight):
        home, r = divmod(j, eight)
        pivot = tiles[home][:, r : r + 1, :]
        scale = lax.rsqrt(pivot[:, :, j : j + 1])
        scaled = pivot * scale
        step = scaled * scale
        for t in range(home, len(tiles)):
            column = tiles[t][:, :, j : j + 1]
            if t == home:
                if r < eight - 1:
                    below = jnp.where(row_of > r, column, 0.0)
                    tiles[t] = tiles[t] - below * step
                tiles[t] = jnp.where(row_of == r, scaled, tiles[t])
            else:
                tiles[t] = tiles[t] - column * step
    return tiles


def factor_refs(sums, out_ref, first):
    width = sums[0].shape[0]
    rows = lax.broadcasted_iota(jnp.int32, (width, width), 0)
    cols = lax.broadcasted_iota(jnp.int32, (width, width), 1)
    eye = (rows == cols).astype(jnp.float32)
    whole = jnp.stack([jnp.concatenate([s, eye], axis=1) for s in sums])
    tiles = eliminate([whole[:, 8 * t : 8 * t + 8, :] for t in range(width // 8)])
    for t, tile in enumerate(tiles):
        lane = lax.broadcasted_iota(jnp.int32, tile.shape, 2)
        row = lax.broadcasted_iota(jnp.int32, tile.shape, 1) + 8 * t
        out_ref[pl.ds(first, len(sums)), 8 * t : 8 * t + 8, :] = jnp.where(lane >= row, tile, 0.0)


def factor_kernel(basis_ref, factor_ref):
    sums = []
    for n in range(basis_ref.shape[0]):
        high, low = split(basis_ref[n])
        cross = mul(high, low, NT)
        sums.append(mul(high, high, NT) + cross + mul(low, high, NT))
    factor_refs(sums, factor_ref, 0)


def unpack_rows(rows_ref, scratch, first, count, width):
    for m in range(width // 2):
        both = rows_ref[pl.ds(first, count), 2 * m * width : 2 * (m + 1) * width]
        scratch[pl.ds(2 * m, count, stride=width), :] = both
        scratch[pl.ds(2 * m + 1, count, stride=width), :] = pltpu.roll(both, width, 1)


def pack_rows(scratch, rows_ref, first, count, width):
    lane = lax.broadcasted_iota(jnp.int32, (count, 2 * width), 1)
    for m in range(width // 2):
        even = scratch[pl.ds(2 * m, count, stride=width), :]
        odd = scratch[pl.ds(2 * m + 1, count, stride=width), :]
        rows_ref[pl.ds(first, count), 2 * m * width : 2 * (m + 1) * width] = jnp.where(
            lane < width, even, pltpu.roll(odd, width, 1)
        )


def ortho_kernel(scale, basis_ref, factor_ref, ortho_ref):
    width = factor_ref.shape[1]
    for n in range(basis_ref.shape[0]):
        inverse = factor_ref[n][:, width:] * scale
        ortho_ref[n] = exact_mul(inverse, basis_ref[n], NN)


def level_kernel(factor_ref, leaf_ref, upper_ref, new_leaf_ref, raised_ref, inner_ref,
                 scratch, lifted, level_one):
    leaves, width = factor_ref.shape[0], factor_ref.shape[1]
    clusters = leaves // 2
    for first in range(0, leaves, 8):
        unpack_rows(leaf_ref, scratch, first, 8, width)
        for i in range(8):
            lifted[first + i] = exact_mul(
                factor_ref[first + i][:, :width], scratch[i * width : (i + 1) * width, :width], NN
            )
    sums = []
    for c in range(clusters):
        pair = split(jnp.concatenate([lifted[2 * c], lifted[2 * c + 1]], axis=0))
        sums.append(split_mul(pair, pair, TN))
    factor_refs(sums, level_one, 0)
    for first in range(0, leaves, 8):
        for i in range(8):
            n = first + i
            scratch[i * width : (i + 1) * width, :width] = exact_mul(
                lifted[n], level_one[n // 2][:, width:], NT
            )
        pack_rows(scratch, new_leaf_ref, first, 8, width)
    unpack_rows(upper_ref, scratch, 0, clusters, width)
    for c in range(clusters):
        up = exact_mul(level_one[c][:, :width], scratch[c * width : (c + 1) * width, :width], NN)
        raised_ref[c] = up
        both = split(up)
        inner_ref[c] = split_mul(both, both, TN)


def upper_kernel(raised_ref, inner_ref, partner_ref, new_upper_ref, scratch, level_two):
    clusters, width = raised_ref.shape[0], raised_ref.shape[1]
    factor_refs([inner_ref[c] + partner_ref[c] for c in range(clusters)], level_two, 0)
    for c in range(clusters):
        scratch[c * width : (c + 1) * width, :width] = exact_mul(
            raised_ref[c], level_two[c][:, width:], NT
        )
    pack_rows(scratch, new_upper_ref, 0, clusters, width)


def left_kernel(row_ref, factor_ref, coupling_ref, left_ref, scratch):
    width = factor_ref.shape[1]

    @pl.loop(0, coupling_ref.shape[0] // 8)
    def _(g):
        first = pl.multiple_of(g * 8, 8)
        unpack_rows(coupling_ref, scratch, first, 8, width)
        for i in range(8):
            factor = factor_ref[row_ref[first + i]][:, :width]
            left_ref[first + i] = exact_mul(factor, scratch[i * width : (i + 1) * width, :width], NN)


def right_kernel(col_ref, table_ref, left_ref, out_ref, scratch, picked, sems):
    blocks, width = left_ref.shape[0], left_ref.shape[1]

    @pl.loop(0, blocks // 8)
    def _(g):
        for i in range(8):
            b = g * 8 + i
            pltpu.make_async_copy(table_ref.at[col_ref[b]], picked.at[b], sems.at[g]).start()

    @pl.loop(0, blocks // 8)
    def _(g):
        first = pl.multiple_of(g * 8, 8)
        pltpu.make_async_copy(
            table_ref.at[pl.ds(0, 8)], picked.at[pl.ds(first, 8)], sems.at[g]
        ).wait()
        for i in range(8):
            factor = picked[first + i]
            scratch[i * width : (i + 1) * width, :width] = exact_mul(left_ref[first + i], factor, NT)
        pack_rows(scratch, out_ref, first, 8, width)


def call(kernel, outs, args, scratch=(), smem=(), flops=0, far=(), sems=0):
    spec = pl.BlockSpec(memory_space=pltpu.VMEM)
    scalar = pl.BlockSpec(memory_space=pltpu.SMEM)
    outs = [jax.ShapeDtypeStruct(shape, jnp.float32) for shape in outs]
    moved = 4 * sum(math.prod(a.shape) for a in (*args, *outs))
    return pl.pallas_call(
        kernel,
        out_shape=outs,
        in_specs=[scalar] * len(smem)
        + [pl.BlockSpec(memory_space=pl.ANY)] * len(far)
        + [spec] * len(args),
        out_specs=[spec] * len(outs),
        scratch_shapes=[pltpu.VMEM(shape, jnp.float32) for shape in scratch]
        + [pltpu.SemaphoreType.DMA((sems,))] * (sems > 0),
        compiler_params=pltpu.CompilerParams(vmem_limit_bytes=VMEM_BYTES),
        cost_estimate=pl.CostEstimate(flops=flops, bytes_accessed=moved, transcendentals=0),
    )(*smem, *far, *args)


def shards(axes, basis, leaf_transfer, upper_transfer, coupling, row_leaf, col_dev, col_leaf):
    leaves, width, points = basis.shape
    clusters, blocks = upper_transfer.shape[0], coupling.shape[0]
    group = min(GROUP, leaves)
    factors = pl.pallas_call(
        factor_kernel,
        grid=(leaves // group,),
        out_shape=jax.ShapeDtypeStruct((leaves, width, 2 * width), jnp.float32),
        in_specs=[pl.BlockSpec((group, width, points), lambda g: (g, 0, 0))],
        out_specs=pl.BlockSpec((group, width, 2 * width), lambda g: (g, 0, 0)),
        compiler_params=pltpu.CompilerParams(vmem_limit_bytes=VMEM_BYTES),
    )(basis)
    table = lax.all_gather(factors[:, :, :width], axes, axis=0, tiled=True)
    ortho = pl.pallas_call(
        functools.partial(ortho_kernel, math.sqrt(points)),
        grid=(leaves // 4,),
        out_shape=jax.ShapeDtypeStruct(basis.shape, jnp.float32),
        in_specs=[
            pl.BlockSpec((4, width, points), lambda g: (g, 0, 0)),
            pl.BlockSpec((4, width, 2 * width), lambda g: (g, 0, 0)),
        ],
        out_specs=pl.BlockSpec((4, width, points), lambda g: (g, 0, 0)),
        compiler_params=pltpu.CompilerParams(vmem_limit_bytes=VMEM_BYTES),
        cost_estimate=pl.CostEstimate(
            flops=6 * basis.size * width, bytes_accessed=8 * basis.size, transcendentals=0
        ),
    )(basis, factors)
    square = (width, 2 * width)
    new_leaf, raised, inner = call(
        level_kernel,
        [leaf_transfer.shape, (clusters, width, width), (clusters, width, width)],
        [factors, leaf_transfer, upper_transfer],
        scratch=[(8 * width, 2 * width), (leaves, width, width), (clusters, *square)],
        flops=10**9,
    )
    size = lax.axis_size(axes[0])
    partner = lax.ppermute(inner, axes[0], [(i, i ^ 1) for i in range(size)])
    (left,) = call(
        left_kernel,
        [(blocks, width, width)],
        [factors, coupling],
        scratch=[(8 * width, 2 * width)],
        smem=[row_leaf],
        flops=10**9,
    )
    (new_upper,) = call(
        upper_kernel,
        [upper_transfer.shape],
        [raised, inner, partner],
        scratch=[(8 * width, 2 * width), (clusters, *square)],
        flops=10**9,
    )
    (coupling_out,) = call(
        right_kernel,
        [coupling.shape],
        [left],
        far=[table],
        scratch=[(8 * width, 2 * width), (blocks, width, width)],
        sems=blocks // 8,
        smem=[col_dev[:, 0] * leaves + col_leaf],
        flops=10**9,
    )
    return ortho, new_leaf, new_upper, coupling_out


def solution(mesh):
    axes = tuple(mesh.axis_names)
    in_specs = (
        P(axes, None, None),
        P(axes, None),
        P(axes, None),
        P(axes, None),
        P(axes),
        P(axes, None),
        P(axes),
    )
    out_specs = (P(axes, None, None), P(axes, None), P(axes, None), P(axes, None))
    return jax.shard_map(
        functools.partial(shards, axes),
        mesh=mesh,
        in_specs=in_specs,
        out_specs=out_specs,
        check_vma=False,
    )
```

```python
import functools
import math

import jax
import jax.numpy as jnp
from jax import lax
from jax.experimental import pallas as pl
from jax.experimental.pallas import tpu as pltpu
from jax.sharding import PartitionSpec as P

PANEL = 4
BATCH = 32
NN = (((1,), (0,)), ((), ()))
NT = (((1,), (1,)), ((), ()))
TN = (((0,), (0,)), ((), ()))
VMEM_BYTES = 56 * 1024 * 1024


def split(x):
    high = x.astype(jnp.bfloat16)
    return high, (x - high.astype(jnp.float32)).astype(jnp.bfloat16)


def mul(first, second, dims):
    return lax.dot_general(first, second, dims, preferred_element_type=jnp.float32)


def split_mul(first, second, dims):
    return (
        mul(first[0], second[1], dims)
        + mul(first[1], second[0], dims)
        + mul(first[0], second[0], dims)
    )


def exact_mul(first, second, dims):
    return split_mul(split(first), split(second), dims)


def eliminate(tiles):
    tiles = list(tiles)
    count, eight, lanes = tiles[0].shape
    row_of = lax.broadcasted_iota(jnp.int32, (1, eight, 1), 1)
    for start in range(0, len(tiles) * eight, PANEL):
        home, r0 = divmod(start, eight)
        columns = {
            t: [
                jnp.broadcast_to(tiles[t][:, :, start + q : start + q + 1], tiles[t].shape)
                for q in range(PANEL)
            ]
            for t in range(home, len(tiles))
        }
        for q in range(PANEL):
            r = r0 + q
            scale = lax.rsqrt(columns[home][q][:, r : r + 1, :])
            scaled = tiles[home][:, r : r + 1, :] * scale
            step = scaled * scale
            square = scale * scale
            later = [columns[home][p][:, r : r + 1, :] * square for p in range(q + 1, PANEL)]
            for t in range(home, len(tiles)):
                factor = columns[t][q]
                if t == home:
                    factor = jnp.where(row_of > r, factor, 0.0)
                tiles[t] = tiles[t] - factor * step
                for p in range(q + 1, PANEL):
                    columns[t][p] = columns[t][p] - factor * later[p - q - 1]
            tiles[home] = jnp.where(row_of == r, scaled, tiles[home])
    return tiles


def factor_refs(sums, out_ref, first):
    width = sums[0].shape[0]
    rows = lax.broadcasted_iota(jnp.int32, (width, width), 0)
    cols = lax.broadcasted_iota(jnp.int32, (width, width), 1)
    eye = (rows == cols).astype(jnp.float32)
    whole = jnp.stack([jnp.concatenate([s, eye], axis=1) for s in sums])
    tiles = eliminate([whole[:, 8 * t : 8 * t + 8, :] for t in range(width // 8)])
    for t, tile in enumerate(tiles):
        lane = lax.broadcasted_iota(jnp.int32, tile.shape, 2)
        row = lax.broadcasted_iota(jnp.int32, tile.shape, 1) + 8 * t
        out_ref[pl.ds(first, len(sums)), 8 * t : 8 * t + 8, :] = jnp.where(lane >= row, tile, 0.0)


def packed_pieces(factor):
    width, lanes = factor.shape
    half = width // 2
    rows = lax.broadcasted_iota(jnp.int32, factor.shape, 0)
    cols = lax.broadcasted_iota(jnp.int32, factor.shape, 1)
    diagonal = jnp.sum(jnp.where(rows == cols, factor, 0.0), axis=0, keepdims=True)
    padded = jnp.concatenate([factor[half:], jnp.zeros((lanes - half, lanes), jnp.float32)], axis=0)
    turned = padded.T[half:width]
    rows, cols = rows[:half], cols[:half]
    strict = jnp.where(rows > cols, turned, jnp.where(rows == cols, 0.0, factor[:half]))
    return strict, diagonal


def factor_kernel(basis_ref, factor_ref, packed_ref):
    leaves, width = factor_ref.shape[0], factor_ref.shape[1]
    half = width // 2
    sums = []
    for n in range(leaves):
        high, low = split(basis_ref[n])
        cross = mul(high, low, NT)
        sums.append(mul(high, high, NT) + cross + mul(low, high, NT))
    factor_refs(sums, factor_ref, 0)
    for p in range(leaves // 2):
        first, second = packed_pieces(factor_ref[2 * p]), packed_pieces(factor_ref[2 * p + 1])
        for here, there, at, size in (
            (first[0], second[0], p * half, half),
            (first[1], second[1], leaves // 2 * half + p, 1),
        ):
            lane = lax.broadcasted_iota(jnp.int32, here.shape, 1)
            packed_ref[at : at + size, :] = jnp.where(lane < width, here, pltpu.roll(there, width, 1))


def unpack_rows(rows_ref, scratch, first, count, width, base=0):
    for m in range(width // 2):
        both = rows_ref[pl.ds(first, count), 2 * m * width : 2 * (m + 1) * width]
        scratch[pl.ds(base + 2 * m, count, stride=width), :] = both
        scratch[pl.ds(base + 2 * m + 1, count, stride=width), :] = pltpu.roll(both, width, 1)


def pack_rows(scratch, rows_ref, first, count, width, base=0):
    lane = lax.broadcasted_iota(jnp.int32, (count, 2 * width), 1)
    for m in range(width // 2):
        even = scratch[pl.ds(base + 2 * m, count, stride=width), :]
        odd = scratch[pl.ds(base + 2 * m + 1, count, stride=width), :]
        rows_ref[pl.ds(first, count), 2 * m * width : 2 * (m + 1) * width] = jnp.where(
            lane < width, even, pltpu.roll(odd, width, 1)
        )


def ortho_kernel(scale, basis_ref, factor_ref, ortho_ref):
    width = factor_ref.shape[1]
    for n in range(basis_ref.shape[0]):
        inverse = factor_ref[n][:, width:] * scale
        ortho_ref[n] = exact_mul(inverse, basis_ref[n], NN)


class Gather:
    def __init__(self, axes, mine, table, recv, up, down, stage, other):
        self.grp_size, self.dev_size = lax.axis_size(axes[0]), lax.axis_size(axes[1])
        self.bits = self.grp_size.bit_length() - 1
        self.line = self.dev_size // 2
        self.grp, self.dev = lax.axis_index(axes[0]), lax.axis_index(axes[1])
        self.z, self.core = self.dev // 2, self.dev % 2
        steps = [(1 << i) - 2 * (1 << i) * ((self.grp // (1 << i)) % 2) for i in range(self.bits)]
        self.first_step = steps[0]
        self.steps = [steps[i] + self.core * (steps[-1 - i] - steps[i]) for i in range(self.bits)]
        self.mine, self.table, self.recv = mine, table, recv
        self.up, self.down, self.stage, self.other = up, down, stage, other
        self.slot = self.grp * self.dev_size + self.dev

    def enter(self):
        barrier = pltpu.get_barrier_semaphore()

        def greet(device):
            pl.semaphore_signal(barrier, inc=1, device_id=device, device_id_type=pl.DeviceIdType.MESH)

        greet((self.grp, self.dev + 1 - 2 * self.core))
        for step in self.steps:
            greet((self.grp + step, self.dev))
        pl.when(self.z > 0)(lambda: greet((self.grp, self.dev - 2)))
        pl.when(self.z < self.line - 1)(lambda: greet((self.grp, self.dev + 2)))
        below = (self.z + self.line - 1) // self.line
        above = (2 * self.line - 2 - self.z) // self.line
        pl.semaphore_wait(barrier, 1 + self.bits + below + above)

    def copy(self, slot, sem, device, own=False):
        return pltpu.make_async_remote_copy(
            src_ref=self.mine if own else self.table.at[slot],
            dst_ref=self.table.at[slot],
            send_sem=sem,
            recv_sem=self.recv.at[slot],
            device_id=device,
            device_id_type=pl.DeviceIdType.MESH,
        )

    def to_line(self, slot, z, sign, own=False):
        sem = self.up.at[z] if sign > 0 else self.down.at[z]
        return self.copy(slot, sem, (self.grp, self.dev + 2 * sign), own)

    def room(self, sign):
        return self.z < self.line - 1 if sign > 0 else self.z > 0

    def to_rest(self, slot, z, subset, stage, own=False):
        copies = []
        for s in range(stage, self.bits):
            at = ((1 << s) - 1 + subset) * self.line + z
            copies.append(self.copy(slot, self.stage.at[at], (self.grp + self.steps[s], self.dev), own))
        sibling = (self.grp, self.dev + 1 - 2 * self.core)
        copies.append(self.copy(slot, self.other.at[subset * self.line + z], sibling, own))
        return copies

    def subsets(self, stage):
        if stage == 0:
            return [(0, self.grp)]
        found = []
        for low in range(1 << (stage - 1)):
            number = low + (1 << (stage - 1))
            offset = sum((self.steps[i] for i in range(stage) if number >> i & 1), 0)
            found.append((number, self.grp + offset))
        return found

    def arrivals(self, step):
        for stage in range(self.bits + 1):
            k = step - stage
            if 0 <= k < self.line and (stage, k) != (0, 0):
                for sign in (1, -1) if k else (1,):
                    yield stage, k, sign

    def visit(self, step, act):
        for stage, k, sign in self.arrivals(step):
            z = self.z + sign * k

            def body(stage=stage, k=k, sign=sign, z=z):
                for number, grp in self.subsets(stage):
                    slot = grp * self.dev_size + 2 * z + self.core
                    act(slot, z, stage, number, sign)

            if k == 0:
                body()
            else:
                pl.when((z >= 0) & (z < self.line))(body)

    def pass_on(self, slot, z, stage, number, sign):
        self.copy(slot, self.other.at[0], (self.grp, self.dev + 1 - 2 * self.core)).wait_recv()
        if stage == 0:
            pl.when(self.room(-sign))(lambda: self.to_line(slot, z, -sign).start())
        for copy in self.to_rest(slot, z, number, stage):
            copy.start()

    def settle(self, slot, z, stage, number, sign):
        if stage == 0:
            pl.when(self.room(-sign))(lambda: self.to_line(slot, z, -sign).wait_send())
        for copy in self.to_rest(slot, z, number, stage):
            copy.wait_send()

    def step(self, step):
        if step == 0:
            for sign in (1, -1):
                pl.when(self.room(sign))(lambda sign=sign: self.to_line(self.slot, self.z, sign, True).start())
            for copy in self.to_rest(self.slot, self.z, 0, 0, True):
                copy.start()
        else:
            self.visit(step, self.pass_on)

    def last_step(self):
        return self.line - 1 + self.bits

    def finish(self):
        sibling = (self.grp, self.dev + 1 - 2 * self.core)
        for grp in range(self.grp_size):
            for z in range(self.line):
                slot = grp * self.dev_size + 2 * z + 1 - self.core
                self.copy(slot, self.other.at[0], sibling).wait_recv()
        for sign in (1, -1):
            pl.when(self.room(sign))(lambda sign=sign: self.to_line(self.slot, self.z, sign, True).wait_send())
        for copy in self.to_rest(self.slot, self.z, 0, 0, True):
            copy.wait_send()
        for step in range(1, self.last_step() + 1):
            self.visit(step, self.settle)


def middle_kernel(axes, row_ref, packed_ref, factor_ref, coupling_ref, leaf_ref, upper_ref,
                  table_ref, left_ref, new_leaf_ref, new_upper_ref,
                  scratch, lifted, level, raised, inner, partner, own_sem, pair_sems,
                  recv, up, down, stage, other):
    leaves, width = factor_ref.shape[0], factor_ref.shape[1]
    clusters, blocks = leaves // 2, coupling_ref.shape[0]
    gather = Gather(axes, packed_ref, table_ref, recv, up, down, stage, other)
    gather.enter()
    gather.step(0)
    own = pltpu.make_async_copy(packed_ref, table_ref.at[gather.slot], own_sem)
    own.start()

    for first in range(0, leaves, 8):
        unpack_rows(leaf_ref, scratch, first, 8, width)
        for i in range(8):
            lifted[first + i] = exact_mul(
                factor_ref[first + i][:, :width], scratch[i * width : (i + 1) * width, :width], NN
            )
    sums = []
    for c in range(clusters):
        pair = split(jnp.concatenate([lifted[2 * c], lifted[2 * c + 1]], axis=0))
        sums.append(split_mul(pair, pair, TN))
    gather.step(1)
    factor_refs(sums, level, 0)
    gather.step(2)
    unpack_rows(upper_ref, scratch, 0, clusters, width)
    for c in range(clusters):
        raised[c] = exact_mul(level[c][:, :width], scratch[c * width : (c + 1) * width, :width], NN)
        both = split(raised[c])
        inner[c] = split_mul(both, both, TN)
    exchange = pltpu.make_async_remote_copy(
        src_ref=inner,
        dst_ref=partner,
        send_sem=pair_sems.at[0],
        recv_sem=pair_sems.at[1],
        device_id=(gather.grp + gather.first_step, gather.dev),
        device_id_type=pl.DeviceIdType.MESH,
    )
    exchange.start()
    gather.step(3)
    for first in range(0, leaves, 8):
        for i in range(8):
            n = first + i
            scratch[i * width : (i + 1) * width, :width] = exact_mul(
                lifted[n], level[n // 2][:, width:], NT
            )
        pack_rows(scratch, new_leaf_ref, first, 8, width)

    def lefts(begin, end):
        @pl.loop(begin, end)
        def _(g):
            for sub in range(0, BATCH, 8):
                first = pl.multiple_of(g * BATCH + sub, 8)
                base = sub * width
                unpack_rows(coupling_ref, scratch, first, 8, width, base)
                for i in range(8):
                    at = base + i * width
                    factor = factor_ref[row_ref[first + i]][:, :width]
                    left_ref[first + i] = exact_mul(factor, scratch[at : at + width, :width], NN)

    batches = blocks // BATCH
    lefts(0, batches // 2)
    gather.step(4)
    lefts(batches // 2, batches)
    for step in range(5, gather.last_step() + 1):
        gather.step(step)
    exchange.wait()
    factor_refs([inner[c] + partner[c] for c in range(clusters)], level, 0)
    for c in range(clusters):
        scratch[c * width : (c + 1) * width, :width] = exact_mul(raised[c], level[c][:, width:], NT)
    pack_rows(scratch, new_upper_ref, 0, clusters, width)
    own.wait()
    gather.finish()


def right_kernel(slot_ref, leaf_ref, table_ref, left_ref, out_ref, scratch, picked, diagonals, sems):
    blocks, width = left_ref.shape[0], left_ref.shape[1]
    half = width // 2
    pairs = table_ref.shape[1] // (half + 1)

    @pl.loop(0, blocks // BATCH)
    def _(g):
        for i in range(BATCH):
            b = g * BATCH + i
            slot = slot_ref[b]
            rows = pl.ds(pl.multiple_of(leaf_ref[b] // 2 * half, half), half)
            pltpu.make_async_copy(table_ref.at[slot, rows], picked.at[b], sems.at[g, 0]).start()
            pltpu.make_async_copy(
                table_ref.at[slot, pl.ds(pairs * half, pairs)], diagonals.at[b], sems.at[g, 1]
            ).start()

    rows = lax.broadcasted_iota(jnp.int32, (half, 2 * width), 0)
    cols = lax.broadcasted_iota(jnp.int32, (half, 2 * width), 1)
    empty = jnp.zeros((half, 2 * width), jnp.float32)

    @pl.loop(0, blocks // BATCH)
    def _(g):
        begin = pl.multiple_of(g * BATCH, BATCH)
        pltpu.make_async_copy(
            picked.at[pl.ds(begin, BATCH)], picked.at[pl.ds(begin, BATCH)], sems.at[g, 0]
        ).wait()
        pltpu.make_async_copy(
            diagonals.at[pl.ds(begin, BATCH)], diagonals.at[pl.ds(begin, BATCH)], sems.at[g, 1]
        ).wait()
        for sub in range(0, BATCH, 8):
            first = pl.multiple_of(g * BATCH + sub, 8)
            for i in range(8):
                b = first + i
                odd = leaf_ref[b] % 2 == 1
                strict = picked[b]
                strict = jnp.where(odd, pltpu.roll(strict, width, 1), strict)
                diagonal = diagonals[b, pl.ds(leaf_ref[b] // 2, 1), :]
                diagonal = jnp.where(odd, pltpu.roll(diagonal, width, 1), diagonal)
                top = jnp.where(rows == cols, diagonal, jnp.where((cols >= half) | (rows < cols), strict, 0.0))
                moved = pltpu.roll(strict, half, 1)
                low = jnp.where(rows == cols - half, diagonal, jnp.where(rows > cols - half, moved, 0.0))
                turned = jnp.concatenate([empty, low], axis=0).T
                factor = jnp.concatenate([top[:, :width], turned[half:width]], axis=0)
                at = (sub + i) * width
                scratch[at : at + width, :width] = exact_mul(left_ref[b], factor, NT)
            pack_rows(scratch, out_ref, first, 8, width, sub * width)


def shards(axes, basis, leaf_transfer, upper_transfer, coupling, row_leaf, col_dev, col_leaf):
    leaves, width, points = basis.shape
    clusters, blocks = upper_transfer.shape[0], coupling.shape[0]
    grp_size, dev_size = lax.axis_size(axes[0]), lax.axis_size(axes[1])
    devices, line, bits = grp_size * dev_size, dev_size // 2, grp_size.bit_length() - 1
    packed_rows = leaves // 2 * (width // 2 + 1)
    f32 = jnp.float32
    near = pl.BlockSpec(memory_space=pltpu.VMEM)
    scalar = pl.BlockSpec(memory_space=pltpu.SMEM)
    far = pl.BlockSpec(memory_space=pl.ANY)
    params = functools.partial(pltpu.CompilerParams, vmem_limit_bytes=VMEM_BYTES)

    factors, packed = pl.pallas_call(
        factor_kernel,
        out_shape=[
            jax.ShapeDtypeStruct((leaves, width, 2 * width), f32),
            jax.ShapeDtypeStruct((packed_rows, 2 * width), f32),
        ],
        in_specs=[near],
        out_specs=[near, near],
        compiler_params=params(),
    )(basis)
    table, left, new_leaf, new_upper = pl.pallas_call(
        functools.partial(middle_kernel, axes),
        out_shape=[
            jax.ShapeDtypeStruct((devices, packed_rows, 2 * width), f32),
            jax.ShapeDtypeStruct((blocks, width, width), f32),
            jax.ShapeDtypeStruct(leaf_transfer.shape, f32),
            jax.ShapeDtypeStruct(upper_transfer.shape, f32),
        ],
        in_specs=[scalar, far, near, near, near, near],
        out_specs=[far, near, near, near],
        scratch_shapes=[
            pltpu.VMEM((BATCH * width, 2 * width), f32),
            pltpu.VMEM((leaves, width, width), f32),
            pltpu.VMEM((clusters, width, 2 * width), f32),
            pltpu.VMEM((clusters, width, width), f32),
            pltpu.VMEM((clusters, width, width), f32),
            pltpu.VMEM((clusters, width, width), f32),
            pltpu.SemaphoreType.DMA,
            pltpu.SemaphoreType.DMA((2,)),
            pltpu.SemaphoreType.DMA((devices,)),
            pltpu.SemaphoreType.DMA((line,)),
            pltpu.SemaphoreType.DMA((line,)),
            pltpu.SemaphoreType.DMA((line * (grp_size - 1),)),
            pltpu.SemaphoreType.DMA((line * grp_size,)),
        ],
        compiler_params=params(collective_id=0, has_side_effects=True),
    )(row_leaf, packed, factors, coupling, leaf_transfer, upper_transfer)
    ortho = pl.pallas_call(
        functools.partial(ortho_kernel, math.sqrt(points)),
        grid=(leaves // 4,),
        out_shape=jax.ShapeDtypeStruct(basis.shape, f32),
        in_specs=[
            pl.BlockSpec((4, width, points), lambda g: (g, 0, 0)),
            pl.BlockSpec((4, width, 2 * width), lambda g: (g, 0, 0)),
        ],
        out_specs=pl.BlockSpec((4, width, points), lambda g: (g, 0, 0)),
        compiler_params=params(),
    )(basis, factors)
    coupling_out = pl.pallas_call(
        right_kernel,
        out_shape=jax.ShapeDtypeStruct(coupling.shape, f32),
        in_specs=[scalar, scalar, far, near],
        out_specs=near,
        scratch_shapes=[
            pltpu.VMEM((BATCH * width, 2 * width), f32),
            pltpu.VMEM((blocks, width // 2, 2 * width), f32),
            pltpu.VMEM((blocks, leaves // 2, 2 * width), f32),
            pltpu.SemaphoreType.DMA((blocks // BATCH, 2)),
        ],
        compiler_params=params(),
    )(col_dev[:, 0], col_leaf, table, left)
    return ortho, new_leaf, new_upper, coupling_out


def solution(mesh):
    axes = tuple(mesh.axis_names)
    in_specs = (
        P(axes, None, None),
        P(axes, None),
        P(axes, None),
        P(axes, None),
        P(axes),
        P(axes, None),
        P(axes),
    )
    out_specs = (P(axes, None, None), P(axes, None), P(axes, None), P(axes, None))
    return jax.shard_map(
        functools.partial(shards, axes),
        mesh=mesh,
        in_specs=in_specs,
        out_specs=out_specs,
        check_vma=False,
    )
```

```python
import functools
import math

import jax
import jax.numpy as jnp
from jax import lax
from jax.experimental import pallas as pl
from jax.experimental.pallas import tpu as pltpu
from jax.sharding import PartitionSpec as P

PANEL = 4
BATCH = 32
NN = (((1,), (0,)), ((), ()))
NT = (((1,), (1,)), ((), ()))
TN = (((0,), (0,)), ((), ()))
VMEM_BYTES = 56 * 1024 * 1024


def split(x):
    high = x.astype(jnp.bfloat16)
    return high, (x - high.astype(jnp.float32)).astype(jnp.bfloat16)


def mul(first, second, dims):
    return lax.dot_general(first, second, dims, preferred_element_type=jnp.float32)


def split_mul(first, second, dims):
    return (
        mul(first[0], second[1], dims)
        + mul(first[1], second[0], dims)
        + mul(first[0], second[0], dims)
    )


def exact_mul(first, second, dims):
    return split_mul(split(first), split(second), dims)


def wide_left(x):
    high, low = split(x)
    return jnp.concatenate([high, high, low], axis=1)


def tall_right(x):
    high, low = split(x)
    return jnp.concatenate([high, low, high], axis=0)


def eliminate(tiles):
    tiles = list(tiles)
    count, eight, lanes = tiles[0].shape
    row_of = lax.broadcasted_iota(jnp.int32, (1, eight, 1), 1)
    for start in range(0, len(tiles) * eight, PANEL):
        home, r0 = divmod(start, eight)
        columns = {
            t: [
                jnp.broadcast_to(tiles[t][:, :, start + q : start + q + 1], tiles[t].shape)
                for q in range(PANEL)
            ]
            for t in range(home, len(tiles))
        }
        for q in range(PANEL):
            r = r0 + q
            scale = lax.rsqrt(columns[home][q][:, r : r + 1, :])
            scaled = tiles[home][:, r : r + 1, :] * scale
            step = scaled * scale
            square = scale * scale
            later = [columns[home][p][:, r : r + 1, :] * square for p in range(q + 1, PANEL)]
            for t in range(home, len(tiles)):
                factor = columns[t][q]
                if t == home:
                    factor = jnp.where(row_of > r, factor, 0.0)
                tiles[t] = tiles[t] - factor * step
                for p in range(q + 1, PANEL):
                    columns[t][p] = columns[t][p] - factor * later[p - q - 1]
            tiles[home] = jnp.where(row_of == r, scaled, tiles[home])
    return tiles


def factor_refs(sums, out_ref, first):
    width = sums[0].shape[0]
    rows = lax.broadcasted_iota(jnp.int32, (width, width), 0)
    cols = lax.broadcasted_iota(jnp.int32, (width, width), 1)
    eye = (rows == cols).astype(jnp.float32)
    whole = jnp.stack([jnp.concatenate([s, eye], axis=1) for s in sums])
    tiles = eliminate([whole[:, 8 * t : 8 * t + 8, :] for t in range(width // 8)])
    for t, tile in enumerate(tiles):
        lane = lax.broadcasted_iota(jnp.int32, tile.shape, 2)
        row = lax.broadcasted_iota(jnp.int32, tile.shape, 1) + 8 * t
        out_ref[pl.ds(first, len(sums)), 8 * t : 8 * t + 8, :] = jnp.where(lane >= row, tile, 0.0)


def packed_pieces(factor):
    width, lanes = factor.shape
    half = width // 2
    rows = lax.broadcasted_iota(jnp.int32, factor.shape, 0)
    cols = lax.broadcasted_iota(jnp.int32, factor.shape, 1)
    diagonal = jnp.sum(jnp.where(rows == cols, factor, 0.0), axis=0, keepdims=True)
    padded = jnp.concatenate([factor[half:], jnp.zeros((lanes - half, lanes), jnp.float32)], axis=0)
    turned = padded.T[half:width]
    rows, cols = rows[:half], cols[:half]
    strict = jnp.where(rows > cols, turned, jnp.where(rows == cols, 0.0, factor[:half]))
    return strict, diagonal


def factor_kernel(basis_ref, factor_ref, packed_ref):
    leaves, width = factor_ref.shape[0], factor_ref.shape[1]
    half = width // 2
    sums = []
    for n in range(leaves):
        high, low = split(basis_ref[n])
        cross = mul(high, low, NT)
        sums.append(mul(high, high, NT) + cross + mul(low, high, NT))
    factor_refs(sums, factor_ref, 0)
    for p in range(leaves // 2):
        first, second = packed_pieces(factor_ref[2 * p]), packed_pieces(factor_ref[2 * p + 1])
        for here, there, at, size in (
            (first[0], second[0], p * half, half),
            (first[1], second[1], leaves // 2 * half + p, 1),
        ):
            lane = lax.broadcasted_iota(jnp.int32, here.shape, 1)
            packed_ref[at : at + size, :] = jnp.where(lane < width, here, pltpu.roll(there, width, 1))


def unpack_rows(rows_ref, scratch, first, count, width, base=0):
    for m in range(width // 2):
        both = rows_ref[pl.ds(first, count), 2 * m * width : 2 * (m + 1) * width]
        scratch[pl.ds(base + 2 * m, count, stride=width), :] = both
        scratch[pl.ds(base + 2 * m + 1, count, stride=width), :] = pltpu.roll(both, width, 1)


def pack_rows(scratch, rows_ref, first, count, width, base=0):
    lane = lax.broadcasted_iota(jnp.int32, (count, 2 * width), 1)
    for m in range(width // 2):
        even = scratch[pl.ds(base + 2 * m, count, stride=width), :]
        odd = scratch[pl.ds(base + 2 * m + 1, count, stride=width), :]
        rows_ref[pl.ds(first, count), 2 * m * width : 2 * (m + 1) * width] = jnp.where(
            lane < width, even, pltpu.roll(odd, width, 1)
        )


def ortho_kernel(scale, basis_ref, factor_ref, ortho_ref):
    width = factor_ref.shape[1]
    for n in range(basis_ref.shape[0]):
        inverse = factor_ref[n][:, width:] * scale
        ortho_ref[n] = mul(wide_left(inverse), tall_right(basis_ref[n]), NN)


class Gather:
    def __init__(self, axes, mine, table, recv, up, down, stage, other):
        self.grp_size, self.dev_size = lax.axis_size(axes[0]), lax.axis_size(axes[1])
        self.bits = self.grp_size.bit_length() - 1
        self.line = self.dev_size // 2
        self.grp, self.dev = lax.axis_index(axes[0]), lax.axis_index(axes[1])
        self.z, self.core = self.dev // 2, self.dev % 2
        steps = [(1 << i) - 2 * (1 << i) * ((self.grp // (1 << i)) % 2) for i in range(self.bits)]
        self.first_step = steps[0]
        self.steps = [steps[i] + self.core * (steps[-1 - i] - steps[i]) for i in range(self.bits)]
        self.mine, self.table, self.recv = mine, table, recv
        self.up, self.down, self.stage, self.other = up, down, stage, other
        self.slot = self.grp * self.dev_size + self.dev

    def enter(self):
        barrier = pltpu.get_barrier_semaphore()

        def greet(device):
            pl.semaphore_signal(barrier, inc=1, device_id=device, device_id_type=pl.DeviceIdType.MESH)

        greet((self.grp, self.dev + 1 - 2 * self.core))
        for step in self.steps:
            greet((self.grp + step, self.dev))
        pl.when(self.z > 0)(lambda: greet((self.grp, self.dev - 2)))
        pl.when(self.z < self.line - 1)(lambda: greet((self.grp, self.dev + 2)))
        below = (self.z + self.line - 1) // self.line
        above = (2 * self.line - 2 - self.z) // self.line
        pl.semaphore_wait(barrier, 1 + self.bits + below + above)

    def copy(self, slot, sem, device, own=False):
        return pltpu.make_async_remote_copy(
            src_ref=self.mine if own else self.table.at[slot],
            dst_ref=self.table.at[slot],
            send_sem=sem,
            recv_sem=self.recv.at[slot],
            device_id=device,
            device_id_type=pl.DeviceIdType.MESH,
        )

    def to_line(self, slot, z, sign, own=False):
        sem = self.up.at[z] if sign > 0 else self.down.at[z]
        return self.copy(slot, sem, (self.grp, self.dev + 2 * sign), own)

    def room(self, sign):
        return self.z < self.line - 1 if sign > 0 else self.z > 0

    def to_rest(self, slot, z, subset, stage, own=False):
        copies = []
        for s in range(stage, self.bits):
            at = ((1 << s) - 1 + subset) * self.line + z
            copies.append(self.copy(slot, self.stage.at[at], (self.grp + self.steps[s], self.dev), own))
        sibling = (self.grp, self.dev + 1 - 2 * self.core)
        copies.append(self.copy(slot, self.other.at[subset * self.line + z], sibling, own))
        return copies

    def subsets(self, stage):
        if stage == 0:
            return [(0, self.grp)]
        found = []
        for low in range(1 << (stage - 1)):
            number = low + (1 << (stage - 1))
            offset = sum((self.steps[i] for i in range(stage) if number >> i & 1), 0)
            found.append((number, self.grp + offset))
        return found

    def arrivals(self, step):
        for stage in range(self.bits + 1):
            k = step - stage
            if 0 <= k < self.line and (stage, k) != (0, 0):
                for sign in (1, -1) if k else (1,):
                    yield stage, k, sign

    def visit(self, step, act):
        for stage, k, sign in self.arrivals(step):
            z = self.z + sign * k

            def body(stage=stage, k=k, sign=sign, z=z):
                for number, grp in self.subsets(stage):
                    slot = grp * self.dev_size + 2 * z + self.core
                    act(slot, z, stage, number, sign)

            if k == 0:
                body()
            else:
                pl.when((z >= 0) & (z < self.line))(body)

    def pass_on(self, slot, z, stage, number, sign):
        self.copy(slot, self.other.at[0], (self.grp, self.dev + 1 - 2 * self.core)).wait_recv()
        if stage == 0:
            pl.when(self.room(-sign))(lambda: self.to_line(slot, z, -sign).start())
        for copy in self.to_rest(slot, z, number, stage):
            copy.start()

    def settle(self, slot, z, stage, number, sign):
        if stage == 0:
            pl.when(self.room(-sign))(lambda: self.to_line(slot, z, -sign).wait_send())
        for copy in self.to_rest(slot, z, number, stage):
            copy.wait_send()

    def step(self, step):
        if step == 0:
            for sign in (1, -1):
                pl.when(self.room(sign))(lambda sign=sign: self.to_line(self.slot, self.z, sign, True).start())
            for copy in self.to_rest(self.slot, self.z, 0, 0, True):
                copy.start()
        else:
            self.visit(step, self.pass_on)

    def last_step(self):
        return self.line - 1 + self.bits

    def finish(self):
        sibling = (self.grp, self.dev + 1 - 2 * self.core)
        for grp in range(self.grp_size):
            for z in range(self.line):
                slot = grp * self.dev_size + 2 * z + 1 - self.core
                self.copy(slot, self.other.at[0], sibling).wait_recv()
        for sign in (1, -1):
            pl.when(self.room(sign))(lambda sign=sign: self.to_line(self.slot, self.z, sign, True).wait_send())
        for copy in self.to_rest(self.slot, self.z, 0, 0, True):
            copy.wait_send()
        for step in range(1, self.last_step() + 1):
            self.visit(step, self.settle)


def middle_kernel(axes, row_ref, packed_ref, factor_ref, coupling_ref, leaf_ref, upper_ref,
                  table_ref, left_ref, new_leaf_ref, new_upper_ref,
                  scratch, wide, lifted, level, raised, inner, partner, own_sem, pair_sems,
                  recv, up, down, stage, other):
    leaves, width = factor_ref.shape[0], factor_ref.shape[1]
    clusters, blocks = leaves // 2, coupling_ref.shape[0]
    gather = Gather(axes, packed_ref, table_ref, recv, up, down, stage, other)
    gather.enter()
    gather.step(0)
    own = pltpu.make_async_copy(packed_ref, table_ref.at[gather.slot], own_sem)
    own.start()

    for first in range(0, leaves, 8):
        unpack_rows(leaf_ref, scratch, first, 8, width)
        for i in range(8):
            wide[first + i] = wide_left(factor_ref[first + i][:, :width])
            lifted[first + i] = mul(
                wide[first + i], tall_right(scratch[i * width : (i + 1) * width, :width]), NN
            )
    sums = []
    for c in range(clusters):
        pair = split(jnp.concatenate([lifted[2 * c], lifted[2 * c + 1]], axis=0))
        sums.append(split_mul(pair, pair, TN))
    gather.step(1)
    factor_refs(sums, level, 0)
    gather.step(2)
    unpack_rows(upper_ref, scratch, 0, clusters, width)
    for c in range(clusters):
        raised[c] = exact_mul(level[c][:, :width], scratch[c * width : (c + 1) * width, :width], NN)
        both = split(raised[c])
        inner[c] = split_mul(both, both, TN)
    exchange = pltpu.make_async_remote_copy(
        src_ref=inner,
        dst_ref=partner,
        send_sem=pair_sems.at[0],
        recv_sem=pair_sems.at[1],
        device_id=(gather.grp + gather.first_step, gather.dev),
        device_id_type=pl.DeviceIdType.MESH,
    )
    exchange.start()

    def lefts(begin, end):
        @pl.loop(begin, end)
        def _(g):
            for sub in range(0, BATCH, 8):
                first = pl.multiple_of(g * BATCH + sub, 8)
                base = sub * width
                unpack_rows(coupling_ref, scratch, first, 8, width, base)
                for i in range(8):
                    at = base + i * width
                    left_ref[first + i] = mul(
                        wide[row_ref[first + i]], tall_right(scratch[at : at + width, :width]), NN
                    )

    batches = blocks // BATCH
    lefts(0, batches // 2)
    gather.step(3)
    for first in range(0, leaves, 8):
        for i in range(8):
            n = first + i
            scratch[i * width : (i + 1) * width, :width] = exact_mul(
                lifted[n], level[n // 2][:, width:], NT
            )
        pack_rows(scratch, new_leaf_ref, first, 8, width)
    lefts(batches // 2, batches)
    gather.step(4)
    exchange.wait()
    factor_refs([inner[c] + partner[c] for c in range(clusters)], level, 0)
    for c in range(clusters):
        scratch[c * width : (c + 1) * width, :width] = exact_mul(raised[c], level[c][:, width:], NT)
    pack_rows(scratch, new_upper_ref, 0, clusters, width)
    for step in range(5, gather.last_step() + 1):
        gather.step(step)
    own.wait()
    gather.finish()


def right_kernel(slot_ref, leaf_ref, table_ref, left_ref, leaf_in_ref, upper_in_ref,
                 out_ref, leaf_out_ref, upper_out_ref, scratch):
    blocks, width = left_ref.shape[0], left_ref.shape[1]
    half = width // 2
    pairs = table_ref.shape[1] // (half + 1)
    leaf_out_ref[...] = leaf_in_ref[...]
    upper_out_ref[...] = upper_in_ref[...]
    rows = lax.broadcasted_iota(jnp.int32, (half, 2 * width), 0)
    cols = lax.broadcasted_iota(jnp.int32, (half, 2 * width), 1)
    empty = jnp.zeros((half, 2 * width), jnp.float32)

    @pl.loop(0, blocks // BATCH)
    def _(g):
        for sub in range(0, BATCH, 8):
            first = pl.multiple_of(g * BATCH + sub, 8)
            for i in range(8):
                b = first + i
                odd = leaf_ref[b] % 2 == 1
                slot, pair = slot_ref[b], leaf_ref[b] // 2
                strict = table_ref[slot, pl.ds(pl.multiple_of(pair * half, half), half), :]
                strict = jnp.where(odd, pltpu.roll(strict, width, 1), strict)
                diagonal = table_ref[slot, pl.ds(pairs * half + pair, 1), :]
                diagonal = jnp.where(odd, pltpu.roll(diagonal, width, 1), diagonal)
                top = jnp.where(rows == cols, diagonal, jnp.where((cols >= half) | (rows < cols), strict, 0.0))
                moved = pltpu.roll(strict, half, 1)
                low = jnp.where(rows == cols - half, diagonal, jnp.where(rows > cols - half, moved, 0.0))
                turned = jnp.concatenate([empty, low], axis=0).T
                factor = jnp.concatenate([top[:, :width], turned[half:width]], axis=0)
                at = (sub + i) * width
                scratch[at : at + width, :width] = exact_mul(left_ref[b], factor, NT)
            pack_rows(scratch, out_ref, first, 8, width, sub * width)


def shards(axes, basis, leaf_transfer, upper_transfer, coupling, row_leaf, col_dev, col_leaf):
    leaves, width, points = basis.shape
    clusters, blocks = upper_transfer.shape[0], coupling.shape[0]
    grp_size, dev_size = lax.axis_size(axes[0]), lax.axis_size(axes[1])
    devices, line, bits = grp_size * dev_size, dev_size // 2, grp_size.bit_length() - 1
    packed_rows = leaves // 2 * (width // 2 + 1)
    f32 = jnp.float32
    near = pl.BlockSpec(memory_space=pltpu.VMEM)
    scalar = pl.BlockSpec(memory_space=pltpu.SMEM)
    far = pl.BlockSpec(memory_space=pl.ANY)
    params = functools.partial(pltpu.CompilerParams, vmem_limit_bytes=VMEM_BYTES)

    factors, packed = pl.pallas_call(
        factor_kernel,
        out_shape=[
            jax.ShapeDtypeStruct((leaves, width, 2 * width), f32),
            jax.ShapeDtypeStruct((packed_rows, 2 * width), f32),
        ],
        in_specs=[near],
        out_specs=[near, near],
        compiler_params=params(),
    )(basis)
    table, left, new_leaf, new_upper = pl.pallas_call(
        functools.partial(middle_kernel, axes),
        out_shape=[
            jax.ShapeDtypeStruct((devices, packed_rows, 2 * width), f32),
            jax.ShapeDtypeStruct((blocks, width, width), f32),
            jax.ShapeDtypeStruct(leaf_transfer.shape, f32),
            jax.ShapeDtypeStruct(upper_transfer.shape, f32),
        ],
        in_specs=[scalar, far, near, near, near, near],
        out_specs=[far, near, near, near],
        scratch_shapes=[
            pltpu.VMEM((BATCH * width, 2 * width), f32),
            pltpu.VMEM((leaves, width, 3 * width), jnp.bfloat16),
            pltpu.VMEM((leaves, width, width), f32),
            pltpu.VMEM((clusters, width, 2 * width), f32),
            pltpu.VMEM((clusters, width, width), f32),
            pltpu.VMEM((clusters, width, width), f32),
            pltpu.VMEM((clusters, width, width), f32),
            pltpu.SemaphoreType.DMA,
            pltpu.SemaphoreType.DMA((2,)),
            pltpu.SemaphoreType.DMA((devices,)),
            pltpu.SemaphoreType.DMA((line,)),
            pltpu.SemaphoreType.DMA((line,)),
            pltpu.SemaphoreType.DMA((line * (grp_size - 1),)),
            pltpu.SemaphoreType.DMA((line * grp_size,)),
        ],
        compiler_params=params(collective_id=0, has_side_effects=True),
    )(row_leaf, packed, factors, coupling, leaf_transfer, upper_transfer)
    ortho = pl.pallas_call(
        functools.partial(ortho_kernel, math.sqrt(points)),
        grid=(leaves // 4,),
        out_shape=jax.ShapeDtypeStruct(basis.shape, f32),
        in_specs=[
            pl.BlockSpec((4, width, points), lambda g: (g, 0, 0)),
            pl.BlockSpec((4, width, 2 * width), lambda g: (g, 0, 0)),
        ],
        out_specs=pl.BlockSpec((4, width, points), lambda g: (g, 0, 0)),
        compiler_params=params(),
    )(basis, factors)
    coupling_out, new_leaf, new_upper = pl.pallas_call(
        right_kernel,
        out_shape=[
            jax.ShapeDtypeStruct(coupling.shape, f32),
            jax.ShapeDtypeStruct(new_leaf.shape, f32),
            jax.ShapeDtypeStruct(new_upper.shape, f32),
        ],
        in_specs=[scalar, scalar, near, near, near, near],
        out_specs=[near, near, near],
        scratch_shapes=[pltpu.VMEM((BATCH * width, 2 * width), f32)],
        compiler_params=params(),
    )(col_dev[:, 0], col_leaf, table, left, new_leaf, new_upper)
    return ortho, new_leaf, new_upper, coupling_out


def solution(mesh):
    axes = tuple(mesh.axis_names)
    in_specs = (
        P(axes, None, None),
        P(axes, None),
        P(axes, None),
        P(axes, None),
        P(axes),
        P(axes, None),
        P(axes),
    )
    out_specs = (P(axes, None, None), P(axes, None), P(axes, None), P(axes, None))
    return jax.shard_map(
        functools.partial(shards, axes),
        mesh=mesh,
        in_specs=in_specs,
        out_specs=out_specs,
        check_vma=False,
    )
```
